32 devices in a mesh: row: 4 (over y, core), col: 8 (over z, x).
Axes of the slice: x: 2, y: 2, z: 4, core: 2. Of those that a mesh axis runs over, the one named last changes fastest.
Arguments:
- inputs: bfloat16 [512, 8192], P(None, 'row'), may hold values from -6 to 6
- out_grad: bfloat16 [512, 8192], P(None, 'row'), may hold values from -6 to 6
- gate_weight: bfloat16 [8192, 28672], P('row', 'col'), may hold values from -0.125 to 0.125
- up_weight: bfloat16 [8192, 28672], P('row', 'col'), may hold values from -0.125 to 0.125
- down_weight: bfloat16 [28672, 8192], P('col', 'row'), may hold values from -0.0625 to 0.0625
- gate_mask: int32 [64, 224], P('row', 'col'), may hold values from 0 to 1, as said below
- up_mask: int32 [64, 224], P('row', 'col'), may hold values from 0 to 1, as said below
- down_mask: int32 [224, 64], P('col', 'row'), may hold values from 0 to 1, as said below
Outputs:
- input_grad: bfloat16 [512, 8192], P('col', 'row')
- gate_grad: bfloat16 [8192, 28672], P('row', 'col')
- up_grad: bfloat16 [8192, 28672], P('row', 'col')
- down_grad: bfloat16 [28672, 8192], P('col', 'row')
The draws below stay inside these ranges and needn't reach their ends.
Inputs may be any that keep to these rules, and one draw needn't show every extreme that they name: `gate_mask`: 1 marks a kept 128 x 128 block of the gate projection; the share kept varies over row and column blocks. `up_mask`: 1 marks a kept 128 x 128 block of the up projection; the share kept varies over row and column blocks. `down_mask`: 1 marks a kept 128 x 128 block of the down projection; the share kept varies over row and column blocks.
All inputs are finite; a program needn't handle non-finite values.
Results may differ from the reference program's by a relative error of at most 0.0049.
Values may be sent and summed in bfloat16 or wider, within the bound.
No kernel may reach another device: no remote copies, remote signals or barrier semaphores. Data moves between devices by JAX's collectives and lax.ppermute only.
A program may use at most 256 MiB of HBM per device.

```python
import jax
import jax.numpy as jnp
from jax import lax

D = 8192
FF = 28672
BLOCK = 128
TOKENS = 512
N_ROW = 4
N_COL = 8


def band_mask(key, row_blocks, col_blocks):
    key_rows, key_cols, key_pick = jax.random.split(key, 3)
    row_level = jax.random.randint(key_rows, (row_blocks, 1), 50, 300)
    col_level = jax.random.randint(key_cols, (1, col_blocks), 50, 300)
    rolled = jax.random.randint(key_pick, (row_blocks, col_blocks), 0, 1000)
    return (rolled < row_level + col_level).astype(jnp.int32)


def draw_gate_mask(key, part):
    return band_mask(jax.random.fold_in(key, 11), D // BLOCK, FF // BLOCK)


def draw_up_mask(key, part):
    return band_mask(jax.random.fold_in(key, 23), D // BLOCK, FF // BLOCK)


def draw_down_mask(key, part):
    return band_mask(jax.random.fold_in(key, 37), FF // BLOCK, D // BLOCK)


def shard_levels(rng, dims, pieces, least, high):
    def one(dim, shards_of):
        heights = jax.random.uniform(jax.random.fold_in(jax.random.fold_in(rng, 6), dim), (shards_of,), jnp.float32, least / len(pieces), high / len(pieces))
        return jnp.repeat(jnp.exp(heights), dims[dim] // shards_of).reshape((-1,) + (1,) * (len(dims) - dim - 1))

    level = one(*pieces[0])
    for cut in pieces[1:]:
        level = level * one(*cut)
    return level


def centred(own_key, shape, scale, most, cuts=(), kind=jnp.bfloat16):
    values = scale * jax.random.normal(own_key, shape, jnp.float32)
    if cuts:
        values = values * shard_levels(own_key, shape, cuts, -0.22, 0.18)
    return jnp.clip(values, -most, most).astype(kind)


def setup_inputs(seed: int = 0) -> dict:
    key_of = jax.random.split(jax.random.key(seed), 9)
    inputs = centred(key_of[0], (TOKENS, D), 1.0, 6.0, ((1, 4),))
    out_grad = centred(key_of[1], (TOKENS, D), 1.0, 6.0, ((1, 4),))
    gate_weight = centred(key_of[2], (D, FF), (3 * D // 10) ** -0.5, 0.125, ((0, 4), (1, 8)))
    up_weight = centred(key_of[3], (D, FF), (3 * D // 10) ** -0.5, 0.125, ((0, 4), (1, 8)))
    down_weight = centred(key_of[4], (FF, D), (3 * FF // 10) ** -0.5, 0.0625, ((0, 8), (1, 4)))
    gate_mask = draw_gate_mask(jax.random.fold_in(key_of[8], 71), 0)
    up_mask = draw_up_mask(jax.random.fold_in(key_of[8], 71), 0)
    down_mask = draw_down_mask(jax.random.fold_in(key_of[8], 71), 0)
    return {"inputs": inputs, "out_grad": out_grad, "gate_weight": gate_weight, "up_weight": up_weight, "down_weight": down_weight, "gate_mask": gate_mask, "up_mask": up_mask, "down_mask": down_mask}


def spread(values, keep_mask):
    row_blocks, col_blocks = keep_mask.shape
    row_size = values.shape[0] // row_blocks
    col_size = values.shape[1] // col_blocks
    shaped = values.reshape(row_blocks, row_size, col_blocks, col_size)
    return (shaped * keep_mask.astype(values.dtype)[:, None, :, None]).reshape(values.shape)


def grouped_sum(pairs, groups):
    left, right, left_dim, right_dim = pairs[0]
    width = left.shape[left_dim] // groups
    out_rows = left.shape[1 - left_dim]
    out_cols = right.shape[1 - right_dim]

    def add_group(index, total):
        start = index.astype(jnp.int32) * jnp.int32(width)
        term = jnp.zeros((out_rows, out_cols), jnp.float32)
        for former, latter, former_dim, latter_dim in pairs:
            former_part = lax.dynamic_slice_in_dim(former, start, width, former_dim)
            latter_part = lax.dynamic_slice_in_dim(latter, start, width, latter_dim)
            term = term + lax.dot_general(former_part, latter_part, (((former_dim,), (latter_dim,)), ((), ())), preferred_element_type=jnp.float32)
        return total + term

    return lax.fori_loop(0, groups, add_group, jnp.zeros((out_rows, out_cols), jnp.float32))


def masked_product(former, latter, keep_mask):
    panel_count = N_COL
    width = latter.shape[1] // panel_count
    latter_panels = latter.reshape(latter.shape[0], panel_count, width).transpose(1, 0, 2)
    mask_panels = keep_mask.reshape(keep_mask.shape[0], panel_count, keep_mask.shape[1] // panel_count).transpose(1, 0, 2)

    def one_panel(operands):
        product = jnp.dot(former.T, operands[0], preferred_element_type=jnp.float32)
        return spread(product, operands[1]).astype(jnp.bfloat16)

    stacked = lax.map(one_panel, (latter_panels, mask_panels))
    return stacked.transpose(1, 0, 2).reshape(former.shape[1], latter.shape[1])


def reference(inputs, out_grad, gate_weight, up_weight, down_weight, gate_mask, up_mask, down_mask):
    gate_full = spread(gate_weight, gate_mask)
    up_full = spread(up_weight, up_mask)
    down_full = spread(down_weight, down_mask)
    gate_sum = grouped_sum([(inputs, gate_full, 1, 0)], N_ROW)
    up_sum = grouped_sum([(inputs, up_full, 1, 0)], N_ROW)
    back_sum = grouped_sum([(out_grad, down_full, 1, 1)], N_ROW)
    sigmoid_gate = jax.nn.sigmoid(gate_sum)
    hidden = (gate_sum * sigmoid_gate * up_sum).astype(jnp.bfloat16)
    slope = sigmoid_gate * (1.0 + gate_sum * (1.0 - sigmoid_gate))
    gate_delta = (back_sum * up_sum * slope).astype(jnp.bfloat16)
    up_delta = (back_sum * gate_sum * sigmoid_gate).astype(jnp.bfloat16)
    input_grad = grouped_sum([(gate_delta, gate_full, 1, 1), (up_delta, up_full, 1, 1)], N_COL).astype(jnp.bfloat16)
    gate_grad = masked_product(inputs, gate_delta, gate_mask)
    up_grad = masked_product(inputs, up_delta, up_mask)
    down_grad = masked_product(hidden, out_grad, down_mask)
    return (input_grad, gate_grad, up_grad, down_grad)
```

```python
import jax
import jax.numpy as jnp
from jax import lax
from jax.experimental import pallas as pl
from jax.experimental.pallas import tpu as pltpu
from jax.sharding import PartitionSpec as P

BLOCK = 128
TILE = 256
VMEM_LIMIT = 50 * 1024 * 1024
F32 = jnp.float32
BF16 = jnp.bfloat16
ANY = pl.BlockSpec(memory_space=pl.ANY)


def cost():
    return pl.CostEstimate(flops=10**8, bytes_accessed=10**5, transcendentals=0)


def params():
    return pltpu.CompilerParams(vmem_limit_bytes=VMEM_LIMIT)


def put_masked(out_ref, w_ref, mask_ref, row_base, col_base):
    rows, cols = w_ref.shape
    for i in range(rows // BLOCK):
        for j in range(cols // BLOCK):
            r, c = slice(i * BLOCK, (i + 1) * BLOCK), slice(j * BLOCK, (j + 1) * BLOCK)
            keep = mask_ref[row_base + i, col_base + j] != 0
            block = w_ref[r, c]
            out_ref[r, c] = jnp.where(keep, block, jnp.zeros_like(block))


def cols_spec(rows, first):
    return pl.BlockSpec((rows, TILE), lambda n, *_: (0, n + first))


def rows_spec(cols, first):
    return pl.BlockSpec((TILE, cols), lambda n, *_: (n + first, 0))


def whole_spec(shape, once=False):
    mode = {"pipeline_mode": pl.Buffered(1)} if once else {}
    return pl.BlockSpec(shape, lambda n, *_: (0,) * len(shape), **mode)


def forward(core, x, g, weights, masks, first, tiles, n_pair, deps):
    tokens, d = x.shape
    own = tokens // 2
    per_col = own // n_pair

    def kernel(core_ref, gm, um, dm, x_ref, g_ref, gw_ref, uw_ref, dw_ref, *rest):
        keep_ref, give_ref, gs, us, ds = rest[len(deps) :]
        c0 = (pl.program_id(0) + first) * (TILE // BLOCK)
        low = core_ref[0] == 0

        def put(k, sums):
            top, bottom = sums[:own], sums[own:]
            keep_ref[0, k] = jnp.where(low, top, bottom).reshape(n_pair, per_col, TILE)
            give_ref[0, k] = jnp.where(low, bottom, top).astype(give_ref.dtype).reshape(n_pair, per_col, TILE)

        put_masked(gs, gw_ref, gm, 0, c0)
        put_masked(us, uw_ref, um, 0, c0)
        put_masked(ds, dw_ref, dm, c0, 0)
        put(0, jnp.dot(x_ref[...], gs[...], preferred_element_type=F32))
        put(1, jnp.dot(x_ref[...], us[...], preferred_element_type=F32))
        put(2, lax.dot_general(g_ref[...], ds[...], (((1,), (1,)), ((), ())), preferred_element_type=F32))

    shape = (tiles, 3, n_pair, per_col, TILE)
    out_spec = pl.BlockSpec((1, *shape[1:]), lambda n, *_: (n, 0, 0, 0, 0))
    width = tiles * TILE
    return pl.pallas_call(
        kernel,
        grid_spec=pltpu.PrefetchScalarGridSpec(
            num_scalar_prefetch=4,
            grid=(tiles,),
            in_specs=[
                whole_spec((tokens, d), True),
                whole_spec((tokens, d), True),
                cols_spec(d, first),
                cols_spec(d, first),
                rows_spec(d, first),
            ]
            + [ANY] * len(deps),
            out_specs=[out_spec, out_spec],
            scratch_shapes=[pltpu.VMEM((d, TILE), BF16), pltpu.VMEM((d, TILE), BF16), pltpu.VMEM((TILE, d), BF16)],
        ),
        out_shape=[jax.ShapeDtypeStruct(shape, F32), jax.ShapeDtypeStruct(shape, BF16)],
        compiler_params=params(),
        cost_estimate=cost(),
        name="forward",
    )(core, *masks, x, g, *weights, *deps)


def source_spec(array, begin):
    size = array.shape[0]
    return pl.BlockSpec(
        (1, *array.shape[1:]), lambda n, *_: (jnp.clip(n - begin, 0, size - 1), 0, 0, 0, 0)
    )


def backward(core, sources, x, g, weights, masks, first, acc, grads, x_index, wanted, n_col, deps):
    tokens, d = x.shape
    ff = weights[0].shape[1]
    n_pair = n_col // 2
    per_col = tokens // n_col
    sizes = [own.shape[0] for own, _ in sources]
    begins = [sum(sizes[:k]) for k in range(len(sizes))]
    tiles = sum(sizes)
    with_input, with_weight = "input" in wanted, "weight" in wanted
    last = x_index is not None
    over_tokens = (((0,), (0,)), ((), ()))
    over_hidden = (((1,), (1,)), ((), ()))

    def kernel(core_ref, xi, gm, um, dm, *refs):
        n = pl.program_id(0)
        refs = list(refs)
        value_refs = [refs.pop(0) for _ in range(2 * len(sources))]
        if with_weight:
            x_ref, g_ref = refs.pop(0), refs.pop(0)
        if with_input:
            gw_ref, uw_ref = refs.pop(0), refs.pop(0)
        acc_ref = refs.pop(0) if with_input and acc is not None else None
        del refs[: len(deps) + (3 if with_weight and grads is not None else 0)]
        if with_input:
            if last:
                give_ref, keep_ref = refs.pop(0), refs.pop(0)
                total = refs.pop()
            else:
                total = refs.pop(0)
        if with_weight:
            gg_ref, ug_ref, dg_ref = refs.pop(0), refs.pop(0), refs.pop(0)
        hidden_s, deltas_s = refs.pop(0), refs.pop(0)
        ws = refs.pop(0) if with_input else None
        c0 = (n + first) * (TILE // BLOCK)
        for s in range(len(sources)):

            @pl.when((n >= begins[s]) & (n < begins[s] + sizes[s]))
            def _():
                for who in range(2):
                    ref = value_refs[2 * s + who]
                    half = core_ref[0] if who == 0 else 1 - core_ref[0]
                    hidden_s[half] = ref[0, 0]
                    deltas_s[half, :, :, :TILE] = ref[0, 1]
                    deltas_s[half, :, :, TILE:] = ref[0, 2]

        deltas = deltas_s[...].reshape(tokens, 2 * TILE)
        if with_input:
            put_masked(ws.at[:, :TILE], gw_ref, gm, 0, c0)
            put_masked(ws.at[:, TILE:], uw_ref, um, 0, c0)

            @pl.when(n == 0)
            def _():
                total[...] = jnp.zeros_like(total) if acc is None else acc_ref[...]

            total[...] += lax.dot_general(deltas, ws[...], over_hidden, preferred_element_type=F32)
            if last:

                @pl.when(n == tiles - 1)
                def _():
                    for p in range(n_pair):
                        give_at = pl.multiple_of((2 * p + 1 - xi[0]) * per_col, 16)
                        keep_at = pl.multiple_of((2 * p + xi[0]) * per_col, 16)
                        give_ref[p] = total[pl.ds(give_at, per_col), :].astype(BF16)
                        keep_ref[p] = total[pl.ds(keep_at, per_col), :]

        if with_weight:
            hidden = hidden_s[...].reshape(tokens, TILE)
            gate = lax.dot_general(x_ref[...], deltas[:, :TILE], over_tokens, preferred_element_type=F32)
            put_masked(gg_ref, gate.astype(BF16), gm, 0, c0)
            up = lax.dot_general(x_ref[...], deltas[:, TILE:], over_tokens, preferred_element_type=F32)
            put_masked(ug_ref, up.astype(BF16), um, 0, c0)
            down = jnp.dot(hidden.T, g_ref[...], preferred_element_type=F32)
            put_masked(dg_ref, down.astype(BF16), dm, c0, 0)

    in_specs, operands, aliases = [], [], {}
    out_specs, out_shape = [], []
    scratch = [pltpu.VMEM((2, n_pair, per_col, TILE), BF16), pltpu.VMEM((2, n_pair, per_col, 2 * TILE), BF16)]
    for pair, begin in zip(sources, begins):
        in_specs += [source_spec(v, begin) for v in pair]
        operands += pair
    if with_weight:
        in_specs += [whole_spec((tokens, d), True)] * 2
        operands += [x, g]
    if with_input:
        in_specs += [cols_spec(d, first), cols_spec(d, first)]
        operands += weights[:2]
        scratch.append(pltpu.VMEM((d, 2 * TILE), BF16))
        if acc is not None:
            in_specs.append(whole_spec((tokens, d), True))
            operands.append(acc)
        if last:
            shape = (n_pair, per_col, d)
            out_specs += [whole_spec(shape), whole_spec(shape)]
            out_shape += [jax.ShapeDtypeStruct(shape, BF16), jax.ShapeDtypeStruct(shape, F32)]
            scratch.append(pltpu.VMEM((tokens, d), F32))
        else:
            out_specs.append(whole_spec((tokens, d)))
            out_shape.append(jax.ShapeDtypeStruct((tokens, d), F32))
    if with_weight:
        if grads is not None:
            for k, e in enumerate(grads):
                aliases[5 + len(operands)] = len(out_shape) + k
                in_specs.append(ANY)
                operands.append(e)
        out_specs += [cols_spec(d, first), cols_spec(d, first), rows_spec(d, first)]
        out_shape += [jax.ShapeDtypeStruct(s, BF16) for s in ((d, ff), (d, ff), (ff, d))]
    in_specs += [ANY] * len(deps)
    operands += deps
    width = tiles * TILE
    outs = pl.pallas_call(
        kernel,
        grid_spec=pltpu.PrefetchScalarGridSpec(
            num_scalar_prefetch=5,
            grid=(tiles,),
            in_specs=in_specs,
            out_specs=out_specs,
            scratch_shapes=scratch,
        ),
        out_shape=out_shape,
        input_output_aliases=aliases,
        compiler_params=params(),
        cost_estimate=cost(),
        name="backward_" + "_".join(wanted),
    )(core, core if x_index is None else x_index, *masks, *operands)
    n_in = (2 if last else 1) if with_input else 0
    return outs[:n_in], outs[n_in:]


def local_grads(sums):
    gate_sum, up_sum, back_sum = sums[:, 0], sums[:, 1], sums[:, 2]
    sigmoid_gate = jax.nn.sigmoid(gate_sum)
    silu = gate_sum * sigmoid_gate
    hidden = silu * up_sum
    slope = sigmoid_gate * (1.0 + gate_sum * (1.0 - sigmoid_gate))
    return jnp.stack([hidden, back_sum * up_sum * slope, back_sum * silu], axis=1).astype(BF16)


def after(token, *arrays):
    return lax.optimization_barrier((*arrays, token))[: len(arrays)]


def plan(tiles):
    if tiles < 14:
        sizes = [1, 2, tiles - 3]
        pieces = [(0, 0, 1), (1, 0, 2), (2, 0, tiles - 3)]
        steps = [("F", 0), ("F", 1), ("S", 0), ("F", 2), ("S", 1), ("L", 0), ("S", 2), ("L", 1), ("B", [0, 1]), ("L", 2), ("I", [2]), ("W", [2])]
        return sizes, pieces, steps
    sizes = [1, 1, 2, 3, 3, tiles - 10]
    pieces = [(0, 0, 1), (1, 0, 1), (2, 0, 2), (3, 0, 3), (4, 0, 3), (5, 0, tiles - 12), (5, tiles - 12, 2)]
    steps = [("F", 0), ("F", 1), ("S", 0), ("F", 2), ("S", 1), ("F", 3), ("S", 2), ("F", 4), ("S", 3), ("F", 5)]
    steps += [("L", 0), ("L", 1), ("S", 4), ("L", 2), ("B", [0, 1, 2]), ("L", 3), ("S", 5), ("B", [3]), ("S", 6)]
    steps += [("L", 4), ("B", [4]), ("L", 5), ("B", [5]), ("L", 6), ("I", [6]), ("W", [6])]
    return sizes, pieces, steps


def build(n_row, n_col):
    n_y = n_row // 2
    n_pair = n_col // 2

    def swap_core(v):
        return lax.ppermute(v, "row", [(i, i ^ 1) for i in range(n_row)])

    def from_y(v):
        return [
            lax.ppermute(v, "row", [(i, (i + 2 * s) % n_row) for i in range(n_row)]) for s in range(1, n_y)
        ]

    def shards(inputs, out_grad, gate_w, up_w, down_w, gate_mask, up_mask, down_mask):
        ff = gate_w.shape[1]
        core_arg = (lax.axis_index("row") % 2).reshape(1).astype(jnp.int32)
        col = lax.axis_index("col")
        x_pos, z_pos = col % 2, col // 2
        x_arg = x_pos.reshape(1).astype(jnp.int32)
        masks = (gate_mask, up_mask, down_mask)
        weights = [gate_w, up_w, down_w]
        sizes, pieces, steps = plan(ff // TILE)
        firsts = [sum(sizes[:c]) for c in range(len(sizes))]
        kept, crossed = {}, {}
        mine, arrived, values = {}, {}, {}
        acc, grads = None, None
        token = None

        for kind, what in steps:
            deps = [] if token is None else [token]
            if kind == "F":
                kept[what], give = forward(
                    core_arg, inputs, out_grad, weights, masks, firsts[what], sizes[what], n_pair, deps
                )
                crossed[what] = swap_core(give)
                token = kept[what]
            elif kind == "S":
                c, at, size = pieces[what]
                keep, cross = after(token, kept[c], crossed[c])
                mine[what] = keep[at : at + size] + cross[at : at + size].astype(F32)
                sent = mine[what].astype(BF16)
                arrived[what] = from_y(sent)
                token = sent
            elif kind == "L":
                total, *others = after(token, mine[what], *arrived[what])
                for other in others:
                    total = total + other.astype(F32)
                own = local_grads(total)
                values[what] = (own, swap_core(own))
                token = own
            else:
                wanted = {"B": ("input", "weight"), "I": ("input",), "W": ("weight",)}[kind]
                c, at, _ = pieces[what[0]]
                part, new = backward(
                    core_arg,
                    [values[i] for i in what],
                    inputs,
                    out_grad,
                    weights,
                    masks,
                    firsts[c] + at,
                    acc,
                    grads,
                    x_arg if kind == "I" else None,
                    wanted,
                    n_col,
                    deps,
                )
                if kind == "I":
                    give, keep = part
                else:
                    grads = new
                    acc = part[0] if part else None
                token = new[0] if new else part[0]

        from_x = lax.ppermute(give, "col", [(j, j ^ 1) for j in range(n_col)])
        keep, from_x = after(token, keep, from_x)
        summed = keep + from_x.astype(F32)
        total = lax.dynamic_index_in_dim(summed, z_pos, 0, keepdims=False)
        for s in range(1, n_pair):
            out = lax.dynamic_index_in_dim(summed, z_pos ^ s, 0, keepdims=False).astype(BF16)
            total = total + lax.ppermute(out, "col", [(j, j ^ (2 * s)) for j in range(n_col)]).astype(F32)
        return (total.astype(BF16), *grads)

    return shards


def solution(mesh):
    placed = (
        P(None, "row"),
        P(None, "row"),
        P("row", "col"),
        P("row", "col"),
        P("col", "row"),
        P("row", "col"),
        P("row", "col"),
        P("col", "row"),
    )
    return jax.shard_map(
        build(mesh.shape["row"], mesh.shape["col"]),
        mesh=mesh,
        in_specs=placed,
        out_specs=(P("col", "row"), P("row", "col"), P("row", "col"), P("col", "row")),
        check_vma=False,
    )
```

```python
import jax
import jax.numpy as jnp
from jax import lax
from jax.experimental import pallas as pl
from jax.experimental.pallas import tpu as pltpu
from jax.sharding import PartitionSpec as P

BLOCK = 128
TILE = 256
VMEM_LIMIT = 40 * 1024 * 1024
F32 = jnp.float32
BF16 = jnp.bfloat16
ANY = pl.BlockSpec(memory_space=pl.ANY)
COSTS = {'F': 8400000, 'B': 16800000, 'I': 8400000, 'W': 8400000}


def cost(kind, tiles):
    return pl.CostEstimate(flops=COSTS[kind] * tiles, bytes_accessed=0, transcendentals=0)


def params():
    return pltpu.CompilerParams(vmem_limit_bytes=VMEM_LIMIT)


def put_masked(out_ref, w_ref, mask_ref, row_base, col_base):
    rows, cols = w_ref.shape
    for i in range(rows // BLOCK):
        for j in range(cols // BLOCK):
            r, c = slice(i * BLOCK, (i + 1) * BLOCK), slice(j * BLOCK, (j + 1) * BLOCK)
            keep = mask_ref[row_base + i, col_base + j] != 0
            block = w_ref[r, c]
            out_ref[r, c] = jnp.where(keep, block, jnp.zeros_like(block))


def cols_spec(rows, first):
    return pl.BlockSpec((rows, TILE), lambda n, *_: (0, n + first))


def rows_spec(cols, first):
    return pl.BlockSpec((TILE, cols), lambda n, *_: (n + first, 0))


def whole_spec(shape, once=False):
    mode = {"pipeline_mode": pl.Buffered(1)} if once else {}
    return pl.BlockSpec(shape, lambda n, *_: (0,) * len(shape), **mode)


def forward(core, x, g, weights, masks, first, tiles, n_pair, deps, arrange):
    tokens, d = x.shape
    own = tokens // 2
    per_col = own // n_pair

    def kernel(core_ref, gm, um, dm, x_ref, g_ref, gw_ref, uw_ref, dw_ref, *rest):
        keep_ref, *give_refs = rest[len(deps) :][:4]
        *arranged, gs, us, ds = rest[len(deps) + 4 :]
        c0 = (pl.program_id(0) + first) * (TILE // BLOCK)
        if arrange:

            @pl.when(pl.program_id(0) == 0)
            def _():
                for to_ref, from_ref in zip(arranged, (x_ref, g_ref)):
                    for who in range(2):
                        half = core_ref[0] if who == 0 else 1 - core_ref[0]
                        at = pl.multiple_of(half * own, own)
                        to_ref[who * own : (who + 1) * own, :] = from_ref[pl.ds(at, own), :]

            x_ref, g_ref = arranged

        def put(k, sums):
            keep_ref[0, k] = sums[:own].reshape(n_pair, per_col, TILE)
            give_refs[k][0] = sums[own:].astype(BF16).reshape(n_pair, per_col, TILE)

        put_masked(gs, gw_ref, gm, 0, c0)
        put_masked(us, uw_ref, um, 0, c0)
        put_masked(ds, dw_ref, dm, c0, 0)
        put(0, jnp.dot(x_ref[...], gs[...], preferred_element_type=F32))
        put(1, jnp.dot(x_ref[...], us[...], preferred_element_type=F32))
        put(2, lax.dot_general(g_ref[...], ds[...], (((1,), (1,)), ((), ())), preferred_element_type=F32))

    shape = (tiles, 3, n_pair, per_col, TILE)
    keep_spec = pl.BlockSpec((1, *shape[1:]), lambda n, *_: (n, 0, 0, 0, 0))
    give_spec = pl.BlockSpec((1, *shape[2:]), lambda n, *_: (n, 0, 0, 0))
    width = tiles * TILE
    return pl.pallas_call(
        kernel,
        grid_spec=pltpu.PrefetchScalarGridSpec(
            num_scalar_prefetch=4,
            grid=(tiles,),
            in_specs=[
                whole_spec((tokens, d), True),
                whole_spec((tokens, d), True),
                cols_spec(d, first),
                cols_spec(d, first),
                rows_spec(d, first),
            ]
            + [ANY] * len(deps),
            out_specs=[keep_spec] + [give_spec] * 3 + [whole_spec((tokens, d))] * (2 * arrange),
            scratch_shapes=[pltpu.VMEM((d, TILE), BF16), pltpu.VMEM((d, TILE), BF16), pltpu.VMEM((TILE, d), BF16)],
        ),
        out_shape=[jax.ShapeDtypeStruct(shape, F32)]
        + [jax.ShapeDtypeStruct((tiles, *shape[2:]), BF16)] * 3
        + [jax.ShapeDtypeStruct((tokens, d), BF16)] * (2 * arrange),
        compiler_params=params(),
        cost_estimate=cost("F", tiles),
        name=f"forward_t{tiles}",
    )(core, *masks, x, g, *weights, *deps)


def source_spec(array, begin):
    size = array.shape[0]
    return pl.BlockSpec(
        (1, *array.shape[1:]), lambda n, *_: (jnp.clip(n - begin, 0, size - 1), 0, 0, 0)
    )


def backward(sources, x, g, weights, masks, first, acc, grads, x_index, wanted, n_col, deps, n_part):
    tokens, d = x.shape
    ff = weights[0].shape[1]
    n_pair = n_col // 2
    per_col = tokens // n_col
    sizes = [own[0].shape[0] for own, _ in sources]
    begins = [sum(sizes[:k]) for k in range(len(sizes))]
    tiles = sum(sizes)
    with_input, with_weight = "input" in wanted, "weight" in wanted
    used = (0, 1, 2) if with_weight else (1, 2)
    last = x_index is not None
    part_rows = per_col // n_part
    over_tokens = (((0,), (0,)), ((), ()))
    over_hidden = (((1,), (1,)), ((), ()))

    def kernel(xi, gm, um, dm, *refs):
        n = pl.program_id(0)
        refs = list(refs)
        value_refs = [[{q: refs.pop(0) for q in used} for _ in range(2)] for _ in sources]
        if with_weight:
            x_ref, g_ref = refs.pop(0), refs.pop(0)
        if with_input:
            gw_ref, uw_ref = refs.pop(0), refs.pop(0)
        acc_ref = refs.pop(0) if with_input and acc is not None else None
        del refs[: len(deps) + (3 if with_weight and grads is not None else 0)]
        if with_input:
            if last:
                give_refs, keep_refs = ([refs.pop(0) for _ in range(n_part)] for _ in range(2))
                total = refs.pop()
            else:
                total = refs.pop(0)
        if with_weight:
            gg_ref, ug_ref, dg_ref = refs.pop(0), refs.pop(0), refs.pop(0)
        hidden_s, deltas_s = refs.pop(0), refs.pop(0)
        ws = refs.pop(0) if with_input else None
        c0 = (n + first) * (TILE // BLOCK)
        for s in range(len(sources)):

            @pl.when((n >= begins[s]) & (n < begins[s] + sizes[s]))
            def _():
                for who in range(2):
                    value = value_refs[s][who]
                    if with_weight:
                        hidden_s[who] = value[0][0]
                    deltas_s[who, :, :, :TILE] = value[1][0]
                    deltas_s[who, :, :, TILE:] = value[2][0]

        deltas = deltas_s[...].reshape(tokens, 2 * TILE)
        if with_input:
            put_masked(ws.at[:, :TILE], gw_ref, gm, 0, c0)
            put_masked(ws.at[:, TILE:], uw_ref, um, 0, c0)

            @pl.when(n == 0)
            def _():
                total[...] = jnp.zeros_like(total) if acc is None else acc_ref[...]

            total[...] += lax.dot_general(deltas, ws[...], over_hidden, preferred_element_type=F32)
            if last:

                @pl.when(n == tiles - 1)
                def _():
                    for p in range(n_pair):
                        for q in range(n_part):
                            give_at = pl.multiple_of((2 * p + 1 - xi[0]) * per_col + q * part_rows, 16)
                            keep_at = pl.multiple_of((2 * p + xi[0]) * per_col + q * part_rows, 16)
                            give_refs[q][p] = total[pl.ds(give_at, part_rows), :].astype(BF16)
                            keep_refs[q][p] = total[pl.ds(keep_at, part_rows), :]

        if with_weight:
            hidden = hidden_s[...].reshape(tokens, TILE)
            gate = lax.dot_general(x_ref[...], deltas[:, :TILE], over_tokens, preferred_element_type=F32)
            put_masked(gg_ref, gate.astype(BF16), gm, 0, c0)
            up = lax.dot_general(x_ref[...], deltas[:, TILE:], over_tokens, preferred_element_type=F32)
            put_masked(ug_ref, up.astype(BF16), um, 0, c0)
            down = jnp.dot(hidden.T, g_ref[...], preferred_element_type=F32)
            put_masked(dg_ref, down.astype(BF16), dm, c0, 0)

    in_specs, operands, aliases = [], [], {}
    out_specs, out_shape = [], []
    scratch = [pltpu.VMEM((2, n_pair, per_col, TILE), BF16), pltpu.VMEM((2, n_pair, per_col, 2 * TILE), BF16)]
    for pair, begin in zip(sources, begins):
        for value in pair:
            in_specs += [source_spec(value[q], begin) for q in used]
            operands += [value[q] for q in used]
    if with_weight:
        in_specs += [whole_spec((tokens, d), True)] * 2
        operands += [x, g]
    if with_input:
        in_specs += [cols_spec(d, first), cols_spec(d, first)]
        operands += weights[:2]
        scratch.append(pltpu.VMEM((d, 2 * TILE), BF16))
        if acc is not None:
            in_specs.append(whole_spec((tokens, d), True))
            operands.append(acc)
        if last:
            shape = (n_pair, part_rows, d)
            out_specs += [whole_spec(shape)] * (2 * n_part)
            out_shape += [jax.ShapeDtypeStruct(shape, t) for t in (BF16, F32) for _ in range(n_part)]
            scratch.append(pltpu.VMEM((tokens, d), F32))
        else:
            out_specs.append(whole_spec((tokens, d)))
            out_shape.append(jax.ShapeDtypeStruct((tokens, d), F32))
    if with_weight:
        if grads is not None:
            for k, e in enumerate(grads):
                aliases[4 + len(operands)] = len(out_shape) + k
                in_specs.append(ANY)
                operands.append(e)
        out_specs += [cols_spec(d, first), cols_spec(d, first), rows_spec(d, first)]
        out_shape += [jax.ShapeDtypeStruct(s, BF16) for s in ((d, ff), (d, ff), (ff, d))]
    in_specs += [ANY] * len(deps)
    operands += deps
    width = tiles * TILE
    outs = pl.pallas_call(
        kernel,
        grid_spec=pltpu.PrefetchScalarGridSpec(
            num_scalar_prefetch=4,
            grid=(tiles,),
            in_specs=in_specs,
            out_specs=out_specs,
            scratch_shapes=scratch,
        ),
        out_shape=out_shape,
        input_output_aliases=aliases,
        compiler_params=params(),
        cost_estimate=cost("B" if len(wanted) == 2 else wanted[0][0].upper(), tiles),
        name="backward_" + "_".join(wanted) + f"_t{tiles}",
    )(jnp.zeros((1,), jnp.int32) if x_index is None else x_index, *masks, *operands)
    n_in = (2 * n_part if last else 1) if with_input else 0
    return outs[:n_in], outs[n_in:]


def local_grads(sums):
    gate_sum, up_sum, back_sum = sums[:, 0], sums[:, 1], sums[:, 2]
    sigmoid_gate = jax.nn.sigmoid(gate_sum)
    silu = gate_sum * sigmoid_gate
    hidden = silu * up_sum
    slope = sigmoid_gate * (1.0 + gate_sum * (1.0 - sigmoid_gate))
    return tuple(v.astype(BF16) for v in (hidden, back_sum * up_sum * slope, back_sum * silu))


def after(token, *arrays):
    return lax.optimization_barrier((*arrays, token))[: len(arrays)]


def plan(tiles):
    if tiles < 14:
        sizes = [1, 2, tiles - 3]
        pieces = [(0, 0, 1), (1, 0, 2), (2, 0, tiles - 3)]
        steps = (
        "F0", "F1", "S0", "F2", "S1", "L0", "S2", "L1", "I0,1", "L2", "E2", "W0,1", "X0", "W2",
    )
        return sizes, pieces, steps, 1
    sizes = [1, 2, 3, 3, 3, 2]
    pieces = [(0, 0, 1), (1, 0, 2), (2, 0, 3), (3, 0, 3), (4, 0, 3), (5, 0, 2)]
    steps = (
        "F0", "S0", "F1", "S1", "F2", "F3", "L0", "S2", "F4", "L1", "S3", "F5", "I0,1", "L2", "S4", "W0,1",
        "I2", "L3", "S5", "I3", "L4", "I4", "L5", "E5", "W2", "X0", "W3", "X1", "W4,5",
    )
    return sizes, pieces, steps, 2


def build(n_row, n_col):
    n_y = n_row // 2
    n_pair = n_col // 2

    def swap_core(v):
        return lax.ppermute(v, "row", [(i, i ^ 1) for i in range(n_row)])

    def from_y(v):
        return [
            lax.ppermute(v, "row", [(i, (i + 2 * s) % n_row) for i in range(n_row)]) for s in range(1, n_y)
        ]

    def shards(inputs, out_grad, gate_w, up_w, down_w, gate_mask, up_mask, down_mask):
        ff = gate_w.shape[1]
        core_arg = (lax.axis_index("row") % 2).reshape(1).astype(jnp.int32)
        col = lax.axis_index("col")
        x_pos, z_pos = col % 2, col // 2
        flip = core_arg[0] * (n_pair // 2)
        x_arg = x_pos.reshape(1).astype(jnp.int32)
        masks = (gate_mask, up_mask, down_mask)
        weights = [gate_w, up_w, down_w]
        sizes, pieces, steps, n_part = plan(ff // TILE)
        firsts = [sum(sizes[:c]) for c in range(len(sizes))]
        kept, crossed = {}, {}
        mine, arrived, values = {}, {}, {}
        acc, grads = None, None
        token, parts = None, []
        x, g = inputs, out_grad

        for step in steps:
            kind, what = step[0], [int(k) for k in step[1:].split(",")]
            if kind not in "BIEW":
                what = what[0]
            deps = [] if token is None else [token]
            if kind == "F":
                arrange = not kept
                kept[what], *rest = forward(
                    core_arg, x, g, weights, masks, firsts[what], sizes[what], n_pair, deps, arrange
                )
                if arrange:
                    x, g = rest[3:]
                crossed[what] = [swap_core(v) for v in rest[:3]]
                token = kept[what]
            elif kind == "S":
                c, at, size = pieces[what]
                keep, *cross = after(token, kept[c], *crossed[c])
                mine[what] = keep[at : at + size] + jnp.stack([v[at : at + size] for v in cross], axis=1).astype(F32)
                sent = mine[what].astype(BF16)
                arrived[what] = from_y(sent)
                token = sent
            elif kind == "L":
                total, *others = after(token, mine[what], *arrived[what])
                for other in others:
                    total = total + other.astype(F32)
                own = local_grads(total)
                values[what] = (own, tuple(swap_core(v) for v in own))
                token = own[2]
            elif kind == "X":
                keep, cross = after(token, keeps[what], from_x[what])
                summed = keep + cross.astype(F32)
                token = lax.dynamic_index_in_dim(summed, z_pos ^ flip, 0, keepdims=False)
                from_z = []
                for s in range(1, n_pair):
                    out = lax.dynamic_index_in_dim(summed, (z_pos ^ s) ^ flip, 0, keepdims=False).astype(BF16)
                    from_z.append(lax.ppermute(out, "col", [(j, j ^ (2 * s)) for j in range(n_col)]))
                parts.append((token, from_z))
            else:
                wanted = {"B": ("input", "weight"), "I": ("input",), "E": ("input",), "W": ("weight",)}[kind]
                c, at, _ = pieces[what[0]]
                part, new = backward(
                    [values[i] for i in what],
                    x,
                    g,
                    weights,
                    masks,
                    firsts[c] + at,
                    acc,
                    grads,
                    x_arg if kind == "E" else None,
                    wanted,
                    n_col,
                    deps,
                    n_part,
                )
                if new:
                    grads = new
                if kind == "E":
                    gives, keeps = part[:n_part], part[n_part:]
                    from_x = [lax.ppermute(v, "col", [(j, j ^ 1) for j in range(n_col)]) for v in gives]
                elif part:
                    acc = part[0]
                token = new[0] if new else part[0]

        rows = []
        for own, from_z in parts:
            total, *from_z = after(token, own, *from_z)
            for v in from_z:
                total = total + v.astype(F32)
            rows.append(total.astype(BF16))
        return (jnp.concatenate(rows, axis=0), *grads)

    return shards


def solution(mesh):
    placed = (
        P(None, "row"),
        P(None, "row"),
        P("row", "col"),
        P("row", "col"),
        P("col", "row"),
        P("row", "col"),
        P("row", "col"),
        P("col", "row"),
    )
    return jax.shard_map(
        build(mesh.shape["row"], mesh.shape["col"]),
        mesh=mesh,
        in_specs=placed,
        out_specs=(P("col", "row"), P("row", "col"), P("row", "col"), P("col", "row")),
        check_vma=False,
    )
```

```python
import jax
import jax.numpy as jnp
from jax import lax
from jax.experimental import pallas as pl
from jax.experimental.pallas import tpu as pltpu
from jax.sharding import PartitionSpec as P

BLOCK = 128
TILE = 256
VMEM_LIMIT = 40 * 1024 * 1024
F32 = jnp.float32
BF16 = jnp.bfloat16
ANY = pl.BlockSpec(memory_space=pl.ANY)
COSTS = {'F': 8400000, 'B': 16800000, 'I': 8400000, 'W': 8400000}


def cost(kind, tiles):
    return pl.CostEstimate(flops=COSTS[kind] * tiles, bytes_accessed=0, transcendentals=0)


def params():
    return pltpu.CompilerParams(vmem_limit_bytes=VMEM_LIMIT)


def put_masked(out_ref, w_ref, mask_ref, row_base, col_base):
    rows, cols = w_ref.shape
    for i in range(rows // BLOCK):
        for j in range(cols // BLOCK):
            r, c = slice(i * BLOCK, (i + 1) * BLOCK), slice(j * BLOCK, (j + 1) * BLOCK)
            keep = mask_ref[row_base + i, col_base + j] != 0
            block = w_ref[r, c]
            out_ref[r, c] = jnp.where(keep, block, jnp.zeros_like(block))


def cols_spec(rows, first):
    return pl.BlockSpec((rows, TILE), lambda n, *_: (0, n + first))


def rows_spec(cols, first):
    return pl.BlockSpec((TILE, cols), lambda n, *_: (n + first, 0))


def whole_spec(shape, once=False):
    mode = {"pipeline_mode": pl.Buffered(1)} if once else {}
    return pl.BlockSpec(shape, lambda n, *_: (0,) * len(shape), **mode)


def forward(core, x, g, weights, masks, first, tiles, n_pair, deps, arrange):
    tokens, d = x.shape
    own = tokens // 2
    per_col = own // n_pair

    def kernel(core_ref, gm, um, dm, x_ref, g_ref, gw_ref, uw_ref, dw_ref, *rest):
        keep_ref, *give_refs = rest[len(deps) :][:4]
        *arranged, gs, us, ds = rest[len(deps) + 4 :]
        c0 = (pl.program_id(0) + first) * (TILE // BLOCK)
        if arrange:

            @pl.when(pl.program_id(0) == 0)
            def _():
                for to_ref, from_ref in zip(arranged, (x_ref, g_ref)):
                    for who in range(2):
                        half = core_ref[0] if who == 0 else 1 - core_ref[0]
                        at = pl.multiple_of(half * own, own)
                        to_ref[who * own : (who + 1) * own, :] = from_ref[pl.ds(at, own), :]

            x_ref, g_ref = arranged

        def put(k, sums):
            keep_ref[0, k] = sums[:own].reshape(n_pair, per_col, TILE)
            give_refs[k][0] = sums[own:].astype(BF16).reshape(n_pair, per_col, TILE)

        put_masked(gs, gw_ref, gm, 0, c0)
        put_masked(us, uw_ref, um, 0, c0)
        put_masked(ds, dw_ref, dm, c0, 0)
        put(0, jnp.dot(x_ref[...], gs[...], preferred_element_type=F32))
        put(1, jnp.dot(x_ref[...], us[...], preferred_element_type=F32))
        put(2, lax.dot_general(g_ref[...], ds[...], (((1,), (1,)), ((), ())), preferred_element_type=F32))

    shape = (tiles, 3, n_pair, per_col, TILE)
    keep_spec = pl.BlockSpec((1, *shape[1:]), lambda n, *_: (n, 0, 0, 0, 0))
    give_spec = pl.BlockSpec((1, *shape[2:]), lambda n, *_: (n, 0, 0, 0))
    width = tiles * TILE
    return pl.pallas_call(
        kernel,
        grid_spec=pltpu.PrefetchScalarGridSpec(
            num_scalar_prefetch=4,
            grid=(tiles,),
            in_specs=[
                whole_spec((tokens, d), True),
                whole_spec((tokens, d), True),
                cols_spec(d, first),
                cols_spec(d, first),
                rows_spec(d, first),
            ]
            + [ANY] * len(deps),
            out_specs=[keep_spec] + [give_spec] * 3 + [whole_spec((tokens, d))] * (2 * arrange),
            scratch_shapes=[pltpu.VMEM((d, TILE), BF16), pltpu.VMEM((d, TILE), BF16), pltpu.VMEM((TILE, d), BF16)],
        ),
        out_shape=[jax.ShapeDtypeStruct(shape, F32)]
        + [jax.ShapeDtypeStruct((tiles, *shape[2:]), BF16)] * 3
        + [jax.ShapeDtypeStruct((tokens, d), BF16)] * (2 * arrange),
        compiler_params=params(),
        cost_estimate=cost("F", tiles),
        name=f"forward_t{tiles}",
    )(core, *masks, x, g, *weights, *deps)


def source_spec(array, begin):
    size = array.shape[0]
    return pl.BlockSpec(
        (1, *array.shape[1:]), lambda n, *_: (jnp.clip(n - begin, 0, size - 1), 0, 0, 0)
    )


def backward(sources, x, g, weights, masks, first, acc, grads, x_index, wanted, n_col, deps, n_part):
    tokens, d = x.shape
    ff = weights[0].shape[1]
    n_pair = n_col // 2
    per_col = tokens // n_col
    sizes = [own[0].shape[0] for own, _ in sources]
    begins = [sum(sizes[:k]) for k in range(len(sizes))]
    tiles = sum(sizes)
    with_input, with_weight = "input" in wanted, "weight" in wanted
    used = (0, 1, 2) if with_weight else (1, 2)
    last = x_index is not None
    part_rows = per_col // n_part
    over_tokens = (((0,), (0,)), ((), ()))
    over_hidden = (((1,), (1,)), ((), ()))

    def kernel(xi, gm, um, dm, *refs):
        n = pl.program_id(0)
        refs = list(refs)
        value_refs = [[{q: refs.pop(0) for q in used} for _ in range(2)] for _ in sources]
        if with_weight:
            x_ref, g_ref = refs.pop(0), refs.pop(0)
        if with_input:
            gw_ref, uw_ref = refs.pop(0), refs.pop(0)
        acc_ref = refs.pop(0) if with_input and acc is not None else None
        del refs[: len(deps) + (3 if with_weight and grads is not None else 0)]
        if with_input:
            if last:
                give_refs, keep_refs = ([refs.pop(0) for _ in range(n_part)] for _ in range(2))
                total = refs.pop()
            else:
                total = refs.pop(0)
        if with_weight:
            gg_ref, ug_ref, dg_ref = refs.pop(0), refs.pop(0), refs.pop(0)
        hidden_s, deltas_s = refs.pop(0), refs.pop(0)
        ws = refs.pop(0) if with_input else None
        c0 = (n + first) * (TILE // BLOCK)
        for s in range(len(sources)):

            @pl.when((n >= begins[s]) & (n < begins[s] + sizes[s]))
            def _():
                for who in range(2):
                    value = value_refs[s][who]
                    if with_weight:
                        hidden_s[who] = value[0][0]
                    deltas_s[who, :, :, :TILE] = value[1][0]
                    deltas_s[who, :, :, TILE:] = value[2][0]

        deltas = deltas_s[...].reshape(tokens, 2 * TILE)
        if with_input:
            put_masked(ws.at[:, :TILE], gw_ref, gm, 0, c0)
            put_masked(ws.at[:, TILE:], uw_ref, um, 0, c0)

            @pl.when(n == 0)
            def _():
                total[...] = jnp.zeros_like(total) if acc is None else acc_ref[...]

            total[...] += lax.dot_general(deltas, ws[...], over_hidden, preferred_element_type=F32)
            if last:

                @pl.when(n == tiles - 1)
                def _():
                    for p in range(n_pair):
                        for q in range(n_part):
                            give_at = pl.multiple_of((2 * p + 1 - xi[0]) * per_col + q * part_rows, 16)
                            keep_at = pl.multiple_of((2 * p + xi[0]) * per_col + q * part_rows, 16)
                            give_refs[q][p] = total[pl.ds(give_at, part_rows), :].astype(BF16)
                            keep_refs[q][p] = total[pl.ds(keep_at, part_rows), :]

        if with_weight:
            hidden = hidden_s[...].reshape(tokens, TILE)
            gate = lax.dot_general(x_ref[...], deltas[:, :TILE], over_tokens, preferred_element_type=F32)
            put_masked(gg_ref, gate.astype(BF16), gm, 0, c0)
            up = lax.dot_general(x_ref[...], deltas[:, TILE:], over_tokens, preferred_element_type=F32)
            put_masked(ug_ref, up.astype(BF16), um, 0, c0)
            down = jnp.dot(hidden.T, g_ref[...], preferred_element_type=F32)
            put_masked(dg_ref, down.astype(BF16), dm, c0, 0)

    in_specs, operands, aliases = [], [], {}
    out_specs, out_shape = [], []
    scratch = [pltpu.VMEM((2, n_pair, per_col, TILE), BF16), pltpu.VMEM((2, n_pair, per_col, 2 * TILE), BF16)]
    for pair, begin in zip(sources, begins):
        for value in pair:
            in_specs += [source_spec(value[q], begin) for q in used]
            operands += [value[q] for q in used]
    if with_weight:
        in_specs += [whole_spec((tokens, d), True)] * 2
        operands += [x, g]
    if with_input:
        in_specs += [cols_spec(d, first), cols_spec(d, first)]
        operands += weights[:2]
        scratch.append(pltpu.VMEM((d, 2 * TILE), BF16))
        if acc is not None:
            in_specs.append(whole_spec((tokens, d), True))
            operands.append(acc)
        if last:
            shape = (n_pair, part_rows, d)
            out_specs += [whole_spec(shape)] * (2 * n_part)
            out_shape += [jax.ShapeDtypeStruct(shape, t) for t in (BF16, F32) for _ in range(n_part)]
            scratch.append(pltpu.VMEM((tokens, d), F32))
        else:
            out_specs.append(whole_spec((tokens, d)))
            out_shape.append(jax.ShapeDtypeStruct((tokens, d), F32))
    if with_weight:
        if grads is not None:
            for k, e in enumerate(grads):
                aliases[4 + len(operands)] = len(out_shape) + k
                in_specs.append(ANY)
                operands.append(e)
        out_specs += [cols_spec(d, first), cols_spec(d, first), rows_spec(d, first)]
        out_shape += [jax.ShapeDtypeStruct(s, BF16) for s in ((d, ff), (d, ff), (ff, d))]
    in_specs += [ANY] * len(deps)
    operands += deps
    width = tiles * TILE
    outs = pl.pallas_call(
        kernel,
        grid_spec=pltpu.PrefetchScalarGridSpec(
            num_scalar_prefetch=4,
            grid=(tiles,),
            in_specs=in_specs,
            out_specs=out_specs,
            scratch_shapes=scratch,
        ),
        out_shape=out_shape,
        input_output_aliases=aliases,
        compiler_params=params(),
        cost_estimate=cost("B" if len(wanted) == 2 else wanted[0][0].upper(), tiles),
        name="backward_" + "_".join(wanted) + f"_t{tiles}",
    )(jnp.zeros((1,), jnp.int32) if x_index is None else x_index, *masks, *operands)
    n_in = (2 * n_part if last else 1) if with_input else 0
    return outs[:n_in], outs[n_in:]


def local_grads(sums):
    gate_sum, up_sum, back_sum = sums[:, 0], sums[:, 1], sums[:, 2]
    sigmoid_gate = jax.nn.sigmoid(gate_sum)
    silu = gate_sum * sigmoid_gate
    hidden = silu * up_sum
    slope = sigmoid_gate * (1.0 + gate_sum * (1.0 - sigmoid_gate))
    return tuple(v.astype(BF16) for v in (hidden, back_sum * up_sum * slope, back_sum * silu))


def after(token, *arrays):
    return lax.optimization_barrier((*arrays, token))[: len(arrays)]


def plan(tiles):
    if tiles < 14:
        sizes = [1, 2, tiles - 3]
        pieces = [(0, 0, 1), (1, 0, 2), (2, 0, tiles - 3)]
        steps = (
        "F0", "F1", "S0", "F2", "S1", "L0", "S2", "L1", "I0,1", "L2", "E2", "W0,1", "X0", "W2",
    )
        return sizes, pieces, steps, 1
    sizes = [1, 2, 3, 3, 3, 2]
    pieces = [(0, 0, 1), (1, 0, 2), (2, 0, 3), (3, 0, 3), (4, 0, 3), (5, 0, 2)]
    steps = (
        "F0", "S0", "F1", "S1", "F2", "L0", "S2", "F3", "F4", "L1", "S3", "F5", "I0,1", "L2", "S4", "W0,1",
        "I2", "L3", "S5", "I3", "L4", "I4", "L5", "E5", "W2", "X0", "W3", "X1", "W4,5",
    )
    return sizes, pieces, steps, 2


def build(n_row, n_col):
    n_y = n_row // 2
    n_pair = n_col // 2

    def swap_core(v):
        return lax.ppermute(v, "row", [(i, i ^ 1) for i in range(n_row)])

    def from_y(v):
        return [
            lax.ppermute(v, "row", [(i, (i + 2 * s) % n_row) for i in range(n_row)]) for s in range(1, n_y)
        ]

    def shards(inputs, out_grad, gate_w, up_w, down_w, gate_mask, up_mask, down_mask):
        ff = gate_w.shape[1]
        core_arg = (lax.axis_index("row") % 2).reshape(1).astype(jnp.int32)
        col = lax.axis_index("col")
        x_pos, z_pos = col % 2, col // 2
        flip = core_arg[0] * (n_pair // 2)
        x_arg = x_pos.reshape(1).astype(jnp.int32)
        masks = (gate_mask, up_mask, down_mask)
        weights = [gate_w, up_w, down_w]
        sizes, pieces, steps, n_part = plan(ff // TILE)
        firsts = [sum(sizes[:c]) for c in range(len(sizes))]
        kept, crossed = {}, {}
        mine, arrived, values = {}, {}, {}
        acc, grads = None, None
        token, parts = None, []
        x, g = inputs, out_grad

        for step in steps:
            kind, what = step[0], [int(k) for k in step[1:].split(",")]
            if kind not in "BIEW":
                what = what[0]
            deps = [] if token is None else [token]
            if kind == "F":
                arrange = not kept
                kept[what], *rest = forward(
                    core_arg, x, g, weights, masks, firsts[what], sizes[what], n_pair, deps, arrange
                )
                if arrange:
                    x, g = rest[3:]
                crossed[what] = [swap_core(v) for v in rest[:3]]
                token = kept[what]
            elif kind == "S":
                c, at, size = pieces[what]
                keep, *cross = after(token, kept[c], *crossed[c])
                mine[what] = keep[at : at + size] + jnp.stack([v[at : at + size] for v in cross], axis=1).astype(F32)
                sent = mine[what].astype(BF16)
                arrived[what] = from_y(sent)
                token = sent
            elif kind == "L":
                total, *others = after(token, mine[what], *arrived[what])
                for other in others:
                    total = total + other.astype(F32)
                own = local_grads(total)
                values[what] = (own, tuple(swap_core(v) for v in own))
                token = own[2]
            elif kind == "X":
                keep, cross = after(token, keeps[what], from_x[what])
                summed = keep + cross.astype(F32)
                token = lax.dynamic_index_in_dim(summed, z_pos ^ flip, 0, keepdims=False)
                from_z = []
                for s in range(1, n_pair):
                    out = lax.dynamic_index_in_dim(summed, (z_pos ^ s) ^ flip, 0, keepdims=False).astype(BF16)
                    from_z.append(lax.ppermute(out, "col", [(j, j ^ (2 * s)) for j in range(n_col)]))
                parts.append((token, from_z))
            else:
                wanted = {"B": ("input", "weight"), "I": ("input",), "E": ("input",), "W": ("weight",)}[kind]
                c, at, _ = pieces[what[0]]
                part, new = backward(
                    [values[i] for i in what],
                    x,
                    g,
                    weights,
                    masks,
                    firsts[c] + at,
                    acc,
                    grads,
                    x_arg if kind == "E" else None,
                    wanted,
                    n_col,
                    deps,
                    n_part,
                )
                if new:
                    grads = new
                if kind == "E":
                    gives, keeps = part[:n_part], part[n_part:]
                    from_x = [lax.ppermute(v, "col", [(j, j ^ 1) for j in range(n_col)]) for v in gives]
                elif part:
                    acc = part[0]
                token = new[0] if new else part[0]

        rows = []
        for own, from_z in parts:
            total, *from_z = after(token, own, *from_z)
            for v in from_z:
                total = total + v.astype(F32)
            rows.append(total.astype(BF16))
        return (jnp.concatenate(rows, axis=0), *grads)

    return shards


def solution(mesh):
    placed = (
        P(None, "row"),
        P(None, "row"),
        P("row", "col"),
        P("row", "col"),
        P("col", "row"),
        P("row", "col"),
        P("row", "col"),
        P("col", "row"),
    )
    return jax.shard_map(
        build(mesh.shape["row"], mesh.shape["col"]),
        mesh=mesh,
        in_specs=placed,
        out_specs=(P("col", "row"), P("row", "col"), P("row", "col"), P("col", "row")),
        check_vma=False,
    )
```
